32 devices in a mesh: seq: 8 (over z, core), mp: 4 (over y, x).
Axes of the slice: x: 2, y: 2, z: 4, core: 2. Of those that a mesh axis runs over, the one named last changes fastest.
Arguments:
- qkv_owned: bfloat16 [4, 3072, 6144], P('mp', 'seq'), may hold values from -6 to 6, as said below
- owner: int32 [4, 1024], P('mp'), may hold values from 0 to 7, as said below
- band_rows: int32 [4, 8, 4], P('mp'), may hold values from 0 to 7, as said below
- band_cols: int32 [4, 8, 4], P('mp'), may hold values from 0 to 7
- bias: float32 [16, 2], replicated, may hold values from -1.5 to 1.5
- grad_out: bfloat16 [4, 1024, 2048], P('mp', 'seq'), may hold values from -6 to 6
Outputs:
- attended: bfloat16 [4, 1024, 2048], P('mp', 'seq')
- grad_qkv: bfloat16 [4, 3072, 6144], P('mp', 'seq')
- grad_bias: float32 [16, 2], P('seq')
The draws below stay inside these ranges and needn't reach their ends.
Inputs may be any that keep to these rules, and one draw needn't show every extreme that they name: Within the 128 positions p * 128 to p * 128 + 127 of a document, at most 48 name one owner, and in every such shard some owner is named exactly 48 times. band_rows[b, 0] is b; the 8 blocks of band_rows[b] and band_cols[b] are distinct. `qkv_owned`: rows that no position names are not read.
All inputs are finite; a program needn't handle non-finite values.
Results may differ from the reference program's by a relative error of at most 0.04.
Values may be sent and summed in bfloat16 or wider, within the bound.
A program may use at most 128 MiB of HBM per device.

```python
import math
import jax
import jax.numpy as jnp
from jax import lax

HEADS = 16
HEAD_DIM = 128
TOK_DEV = 128
BLOCK = 128
ROW_BLOCKS = 4
COL_BLOCKS = 4
SEQ_LEN = 1024
NBLK = 8
CAP_PAIR = 48
OWN_SLOTS = 384
DOCS = 4
FEAT = 6144
N_SEQ = 8


def owner_table(key):
    keys = jax.random.split(jax.random.fold_in(key, 17), 4)
    candidates = N_SEQ * CAP_PAIR
    cand_owner = jnp.arange(candidates, dtype=jnp.int32) // CAP_PAIR
    prefer = jax.random.randint(keys[0], (DOCS, 1, N_SEQ), 0, 2048)
    noise = jax.random.randint(keys[1], (DOCS, N_SEQ, candidates), 0, 1024)
    forced = jax.random.randint(keys[2], (DOCS, N_SEQ, 1), 0, N_SEQ)
    logit_scores = noise + jnp.take(prefer, cand_owner, axis=2)
    logit_scores = logit_scores + jnp.where(cand_owner[None, None, :] == forced, 4096, 0)
    logit_scores = logit_scores * candidates + jnp.arange(candidates, dtype=jnp.int32)
    chosen = jnp.argsort(-logit_scores, axis=-1)[:, :, :TOK_DEV]
    owners = jnp.take(cand_owner, chosen)
    mixing = jax.random.randint(keys[3], (DOCS, N_SEQ, TOK_DEV), 0, 1 << 20) * TOK_DEV + jnp.arange(TOK_DEV, dtype=jnp.int32)
    shuffle = jnp.argsort(mixing, axis=-1)
    return jnp.take_along_axis(owners, shuffle, axis=-1).reshape(DOCS, SEQ_LEN).astype(jnp.int32)


def band_table(key):
    noise = jax.random.randint(jax.random.fold_in(key, 29), (DOCS, NBLK, NBLK), 0, 1 << 16) * NBLK + jnp.arange(NBLK, dtype=jnp.int32)
    diagonal = jnp.arange(NBLK)[:, None] == jnp.arange(NBLK)[None, :]
    noise = jnp.where(diagonal[None], -1, noise)
    return jnp.argsort(noise, axis=-1)[:, :, :ROW_BLOCKS + COL_BLOCKS].astype(jnp.int32)


def draw_owner(key, part):
    return owner_table(key)


def draw_band_rows(key, part):
    return band_table(key)[:, :, :ROW_BLOCKS]


def draw_band_cols(key, part):
    return band_table(key)[:, :, ROW_BLOCKS:]


def draw_qkv_owned(key, part):
    keys = jax.random.split(jax.random.fold_in(key, 41), 2)
    total = N_SEQ * OWN_SLOTS
    shape = (DOCS, total, 3, HEADS, HEAD_DIM)
    values = jnp.clip(jax.random.normal(keys[1], shape), -6.0, 6.0)
    return values.reshape(DOCS, total, FEAT).astype(jnp.bfloat16)


def shard_levels(rng, extent, cuts, least, largest):
    def one(position, blocks):
        steps = jax.random.uniform(jax.random.fold_in(jax.random.fold_in(rng, 6), position), (blocks,), jnp.float32, least / len(cuts), largest / len(cuts))
        return jnp.repeat(jnp.exp(steps), extent[position] // blocks).reshape((-1,) + (1,) * (len(extent) - position - 1))

    gain = one(*cuts[0])
    for cut in cuts[1:]:
        gain = gain * one(*cut)
    return gain


def centred(rng, dims, spread, most, cuts=(), held_as=jnp.bfloat16):
    gain = shard_levels(rng, dims, cuts, -0.22, 0.18) if cuts else 1.0
    values = jax.random.normal(rng, dims, jnp.float32) * spread * gain
    return jnp.minimum(jnp.maximum(values, -most), most).astype(held_as)


def setup_inputs(seed: int = 0) -> dict:
    splits = jax.random.split(jax.random.key(seed), 7)
    return {
        "qkv_owned": draw_qkv_owned(jax.random.fold_in(splits[6], 71), 0),
        "owner": draw_owner(jax.random.fold_in(splits[6], 71), 0),
        "band_rows": draw_band_rows(jax.random.fold_in(splits[6], 71), 0),
        "band_cols": draw_band_cols(jax.random.fold_in(splits[6], 71), 0),
        "bias": jnp.clip(jax.random.uniform(splits[4], (HEADS, 2), jnp.float32, -1.5, 1.5), -1.5, 1.5),
        "grad_out": centred(splits[5], (DOCS, SEQ_LEN, HEADS * HEAD_DIM), 1.0, 6.0, ((0, 4), (1, 8))),
    }


def source_rows(owner_doc):
    owner_ids = jnp.arange(N_SEQ, dtype=jnp.int32)
    onehot = (owner_doc[:, None] == owner_ids[None, :]).astype(jnp.int32)
    running = jnp.cumsum(onehot, axis=0) - onehot
    return (owner_doc * OWN_SLOTS + lax.optimization_barrier(jnp.sum(running * onehot, axis=1))).astype(jnp.int32)

def blocked(array):
    return array.reshape(NBLK, BLOCK, HEAD_DIM)

def head_core(query, key_rows, value_rows, grad_rows, selected, bias_pair):
    score_scaling = 1.0 / math.sqrt(HEAD_DIM)
    num_sel = ROW_BLOCKS + COL_BLOCKS
    highest_precision = lax.Precision.HIGHEST
    query_tile_block = blocked(query).astype(jnp.float32)
    gradient_per_block = blocked(grad_rows).astype(jnp.float32)
    selected_keys = blocked(key_rows)[selected].reshape(NBLK, num_sel * BLOCK, HEAD_DIM).astype(jnp.float32)
    selected_values = blocked(value_rows)[selected].reshape(NBLK, num_sel * BLOCK, HEAD_DIM).astype(jnp.float32)
    col_kind = jnp.arange(num_sel * BLOCK) >= ROW_BLOCKS * BLOCK
    key_offset_bias = jnp.where(col_kind, bias_pair[1], bias_pair[0])
    logit_scores = jnp.einsum('xtc,xzc->xtz', query_tile_block, selected_keys, precision=highest_precision) * score_scaling + key_offset_bias[None, None, :]
    row_max = lax.optimization_barrier(jnp.max(logit_scores, axis=-1, keepdims=True))
    exp_scores = jnp.exp(logit_scores - row_max)
    weights = exp_scores / lax.optimization_barrier(jnp.sum(exp_scores, axis=-1, keepdims=True))
    reduced_weights = lax.optimization_barrier(weights.astype(jnp.bfloat16)).astype(jnp.float32)
    attention_result = jnp.einsum('ufn,unp->ufp', reduced_weights, selected_values, precision=highest_precision).astype(jnp.bfloat16)
    attn_wide = lax.optimization_barrier(attention_result).astype(jnp.float32)
    row_delta = lax.optimization_barrier(jnp.sum(gradient_per_block * attn_wide, axis=-1, keepdims=True))
    probability_gradient = jnp.einsum('xtc,xzc->xtz', gradient_per_block, selected_values, precision=highest_precision)
    dscore = weights * (probability_gradient - row_delta)
    bias_grad = jnp.stack([jnp.sum(jnp.where(col_kind, 0.0, dscore)), jnp.sum(jnp.where(col_kind, dscore, 0.0))])
    score_gradient_reduced = lax.optimization_barrier(dscore.astype(jnp.bfloat16)).astype(jnp.float32)
    query_gradient = jnp.einsum('ufn,unp->ufp', score_gradient_reduced, selected_keys, precision=highest_precision) * score_scaling
    selected_key_gradient = jnp.einsum('jyt,jyu->jtu', score_gradient_reduced, query_tile_block, precision=highest_precision) * score_scaling
    selected_value_gradient = jnp.einsum('jyt,jyu->jtu', reduced_weights, gradient_per_block, precision=highest_precision)
    block_hot = (selected[:, :, None] == jnp.arange(NBLK, dtype=jnp.int32)[None, None, :]).astype(jnp.float32)
    grad_key = jnp.einsum('bjc,bjtd->ctd', block_hot, selected_key_gradient.reshape(NBLK, num_sel, BLOCK, HEAD_DIM), precision=highest_precision)
    grad_value = jnp.einsum('bjc,bjtd->ctd', block_hot, selected_value_gradient.reshape(NBLK, num_sel, BLOCK, HEAD_DIM), precision=highest_precision)
    return (attention_result.reshape(SEQ_LEN, HEAD_DIM), query_gradient.reshape(SEQ_LEN, HEAD_DIM), grad_key.reshape(SEQ_LEN, HEAD_DIM), grad_value.reshape(SEQ_LEN, HEAD_DIM), bias_grad)

def reference(qkv_owned, owner, band_rows, band_cols, bias, grad_out):

    def one_doc(bundle):
        rows_owned, owner_doc, row_list, col_list, grad_doc = bundle
        source = source_rows(owner_doc)
        gathered = jnp.take(rows_owned, source, axis=0).reshape(SEQ_LEN, 3, HEADS, HEAD_DIM)
        selected = jnp.concatenate([row_list, col_list], axis=1)
        per_head = gathered.transpose(2, 1, 0, 3)
        grad_heads = grad_doc.reshape(SEQ_LEN, HEADS, HEAD_DIM).transpose(1, 0, 2)

        def one_head(entry):
            head_rows, head_grad, bias_pair = entry
            return head_core(head_rows[0], head_rows[1], head_rows[2], head_grad, selected, bias_pair)
        attention_result, query_gradient, grad_key, grad_value, bias_grad = lax.map(one_head, (per_head, grad_heads, bias))
        attended_doc = attention_result.transpose(1, 0, 2).reshape(SEQ_LEN, HEADS * HEAD_DIM)
        grad_all = jnp.stack([query_gradient, grad_key, grad_value], axis=0)
        grad_all = grad_all.transpose(2, 0, 1, 3).reshape(SEQ_LEN, FEAT).astype(jnp.bfloat16)
        owned = jnp.zeros((N_SEQ * OWN_SLOTS, FEAT), jnp.bfloat16).at[source].set(grad_all)
        return (attended_doc, owned, bias_grad)
    attended, grad_qkv, bias_grad = lax.map(one_doc, (qkv_owned, owner, band_rows, band_cols, grad_out))
    return (attended, grad_qkv, lax.optimization_barrier(jnp.sum(bias_grad, axis=0)))
```

```python
import functools
import math

import jax
import jax.numpy as jnp
from jax import lax
from jax.experimental import pallas as pl
from jax.experimental.pallas import tpu as pltpu
from jax.sharding import PartitionSpec as P

HEADS = 16
HEAD_DIM = 128
ROW_BLOCKS = 4
VMEM_LIMIT = 56 * 1024 * 1024


def source_slots(owner_all, slot_count):
    position = jnp.arange(owner_all.shape[0], dtype=jnp.int32)
    same = owner_all[:, None] == owner_all[None, :]
    earlier = position[None, :] < position[:, None]
    return owner_all * slot_count + jnp.sum((same & earlier).astype(jnp.int32), axis=1)


def pack_kernel(slots, q_ref, k_ref, v_ref, g_ref, out_ref):
    out_ref[0, 0:slots, :] = q_ref[...]
    out_ref[0, slots : 2 * slots, :] = k_ref[...]
    out_ref[0, 2 * slots : 3 * slots, :] = v_ref[...]
    out_ref[0, 3 * slots :, :] = g_ref[...]


def pack(cells, grads, head, per_dev, num_dev):
    slots, tok = cells.shape[0], grads.shape[0]

    def part(j):
        return pl.BlockSpec((slots, HEAD_DIM), lambda d: (0, j * HEADS + d * per_dev + head))

    return pl.pallas_call(
        functools.partial(pack_kernel, slots),
        grid=(num_dev,),
        in_specs=[
            part(0),
            part(1),
            part(2),
            pl.BlockSpec((tok, HEAD_DIM), lambda d: (0, d * per_dev + head)),
        ],
        out_specs=pl.BlockSpec((1, 3 * slots + tok, HEAD_DIM), lambda d: (d, 0, 0)),
        out_shape=jax.ShapeDtypeStruct((num_dev, 3 * slots + tok, HEAD_DIM), jnp.bfloat16),
        compiler_params=pltpu.CompilerParams(vmem_limit_bytes=VMEM_LIMIT),
        cost_estimate=pl.CostEstimate(
            flops=0, bytes_accessed=4 * num_dev * (3 * slots + tok) * HEAD_DIM, transcendentals=0
        ),
    )(cells, cells, cells, grads)


def unpack_kernel(*refs):
    out_ref = refs[-1]
    for h, ref in enumerate(refs[:-1]):
        out_ref[:, h * HEAD_DIM : (h + 1) * HEAD_DIM] = ref[0]


def unpack(arrived, slots):
    per_dev, num_dev = len(arrived), arrived[0].shape[0]
    width = per_dev * HEAD_DIM
    return pl.pallas_call(
        unpack_kernel,
        grid=(num_dev, 3),
        in_specs=[pl.BlockSpec((1, slots, HEAD_DIM), lambda s, j: (s, j, 0))] * per_dev,
        out_specs=pl.BlockSpec((slots, width), lambda s, j: (0, j * num_dev + s)),
        out_shape=jax.ShapeDtypeStruct((slots, 3 * num_dev * width), jnp.bfloat16),
        compiler_params=pltpu.CompilerParams(vmem_limit_bytes=VMEM_LIMIT),
        cost_estimate=pl.CostEstimate(
            flops=0, bytes_accessed=4 * slots * 3 * num_dev * width, transcendentals=0
        ),
    )(*arrived)


def dot(a, b, dims):
    return lax.dot_general(a, b, (dims, ((), ())), preferred_element_type=jnp.float32)


def attend_kernel(
    slots, tok, sel_ref, bias_ref, in_ref, col_ref, row_ref, out_ref, sum_ref,
    cells, qkv, ksel, vsel, dkey, dval, grads,
):
    num_dev = in_ref.shape[0]
    num_blocks, num_sel = sel_ref.shape
    total = num_dev * slots
    dim = HEAD_DIM
    scaling = 1.0 / math.sqrt(dim)

    @pl.loop(0, num_dev)
    def _(o):
        start = pl.multiple_of(o * slots, slots)
        for j in range(3):
            cells[pl.ds(start, slots), j * dim : (j + 1) * dim] = in_ref[
                o, j * slots : (j + 1) * slots, :
            ]

    @pl.loop(0, num_blocks)
    def _(b):
        rows = pl.ds(pl.multiple_of(b * tok, tok), tok)
        ids = lax.broadcasted_iota(jnp.int32, (tok, total), 1)
        hot = jnp.where(ids == col_ref[rows, :], 1.0, 0.0).astype(jnp.bfloat16)
        qkv[rows, :] = dot(hot, cells[...], ((1,), (0,))).astype(jnp.bfloat16)

    dkey[...] = jnp.zeros_like(dkey)
    dval[...] = jnp.zeros_like(dval)
    sum_ref[...] = jnp.zeros_like(sum_ref)
    kind = lax.broadcasted_iota(jnp.int32, (1, num_sel * tok), 1) >= ROW_BLOCKS * tok
    offset = jnp.where(kind, bias_ref[0, 1], bias_ref[0, 0])

    @pl.loop(0, num_blocks)
    def _(b):
        rows = pl.ds(pl.multiple_of(b * tok, tok), tok)
        query = qkv[rows, 0:dim]
        grad = in_ref[b, 3 * slots :, :]
        for i in range(num_sel):
            chosen = pl.ds(pl.multiple_of(sel_ref[b, i] * tok, tok), tok)
            ksel[i * tok : (i + 1) * tok, :] = qkv[chosen, dim : 2 * dim]
            vsel[i * tok : (i + 1) * tok, :] = qkv[chosen, 2 * dim : 3 * dim]
        scores = dot(query, ksel[...], ((1,), (1,))) * scaling + offset
        exps = jnp.exp(scores - jnp.max(scores, axis=1, keepdims=True))
        probs = exps * (1.0 / jnp.sum(exps, axis=1, keepdims=True))
        low = probs.astype(jnp.bfloat16)
        result = dot(low, vsel[...], ((1,), (0,))).astype(jnp.bfloat16)
        out_ref[b, 3 * slots :, :] = result
        delta = jnp.sum(
            grad.astype(jnp.float32) * result.astype(jnp.float32), axis=1, keepdims=True
        )
        dscore = probs * (dot(grad, vsel[...], ((1,), (1,))) - delta)
        sum_ref[...] += jnp.sum(dscore.reshape(tok // 8, 8, num_sel * tok), axis=0)
        dlow = dscore.astype(jnp.bfloat16)
        grads[rows, 0:dim] = (dot(dlow, ksel[...], ((1,), (0,))) * scaling).astype(jnp.bfloat16)
        dk = dot(dlow, query, ((0,), (0,))) * scaling
        dv = dot(low, grad, ((0,), (0,)))
        for i in range(num_sel):
            chosen = pl.ds(pl.multiple_of(sel_ref[b, i] * tok, tok), tok)
            dkey[chosen, :] += dk[i * tok : (i + 1) * tok, :]
            dval[chosen, :] += dv[i * tok : (i + 1) * tok, :]

    grads[:, dim : 2 * dim] = dkey[...].astype(jnp.bfloat16)
    grads[:, 2 * dim : 3 * dim] = dval[...].astype(jnp.bfloat16)

    @pl.loop(0, num_dev)
    def _(o):
        ids = lax.broadcasted_iota(jnp.int32, (slots, num_blocks * tok), 0) + o * slots
        hot = jnp.where(ids == row_ref[...], 1.0, 0.0).astype(jnp.bfloat16)
        back = dot(hot, grads[...], ((1,), (0,))).astype(jnp.bfloat16)
        for j in range(3):
            out_ref[o, j * slots : (j + 1) * slots, :] = back[:, j * dim : (j + 1) * dim]


def attend(arrived, source, selected, bias_pair, slots, tok):
    num_dev = arrived.shape[0]
    num_sel = selected.shape[1]
    length = source.shape[0]
    vmem = pl.BlockSpec(memory_space=pltpu.VMEM)
    smem = pl.BlockSpec(memory_space=pltpu.SMEM)
    dim = HEAD_DIM
    flops = 12 * length * num_sel * tok * dim + 12 * length * num_dev * slots * dim
    return pl.pallas_call(
        functools.partial(attend_kernel, slots, tok),
        in_specs=[smem, smem, vmem, vmem, vmem],
        out_specs=[vmem, vmem],
        out_shape=[
            jax.ShapeDtypeStruct(arrived.shape, jnp.bfloat16),
            jax.ShapeDtypeStruct((8, num_sel * tok), jnp.float32),
        ],
        scratch_shapes=[
            pltpu.VMEM((num_dev * slots, 3 * dim), jnp.bfloat16),
            pltpu.VMEM((length, 3 * dim), jnp.bfloat16),
            pltpu.VMEM((num_sel * tok, dim), jnp.bfloat16),
            pltpu.VMEM((num_sel * tok, dim), jnp.bfloat16),
            pltpu.VMEM((length, dim), jnp.float32),
            pltpu.VMEM((length, dim), jnp.float32),
            pltpu.VMEM((length, 3 * dim), jnp.bfloat16),
        ],
        compiler_params=pltpu.CompilerParams(vmem_limit_bytes=VMEM_LIMIT),
        cost_estimate=pl.CostEstimate(
            flops=2 * flops,
            bytes_accessed=4 * arrived.size,
            transcendentals=length * num_sel * tok,
        ),
    )(selected, bias_pair, arrived, source[:, None], source[None, :])


def exchange(array):
    return lax.all_to_all(array, "seq", split_axis=0, concat_axis=0, tiled=True)


def shards(qkv_owned, owner, band_rows, band_cols, bias, grad_out):
    num_dev = lax.axis_size("seq")
    my_index = lax.axis_index("seq")
    slots = qkv_owned.shape[1]
    tok = grad_out.shape[1]
    per_dev = HEADS // num_dev
    cells, grads = qkv_owned[0], grad_out[0]
    arrived = [exchange(pack(cells, grads, h, per_dev, num_dev)) for h in range(per_dev)]
    source = source_slots(owner[0], slots)
    selected = jnp.concatenate([band_rows[0], band_cols[0]], axis=1)
    bias_pair = lax.dynamic_slice_in_dim(bias, my_index * per_dev, per_dev, 0)
    back, sums = [], []
    for h in range(per_dev):
        out, part = attend(arrived[h], source, selected, bias_pair[h : h + 1], slots, tok)
        back.append(exchange(out))
        sums.append(part)
    sums = jnp.stack(sums)
    bias_grad = jnp.stack(
        [
            jnp.sum(sums[:, :, : ROW_BLOCKS * tok], axis=(1, 2)),
            jnp.sum(sums[:, :, ROW_BLOCKS * tok :], axis=(1, 2)),
        ],
        axis=1,
    )
    grad_cells = unpack(back, slots)
    attended = jnp.concatenate(
        [back[h][d, 3 * slots :, :] for d in range(num_dev) for h in range(per_dev)], axis=1
    )
    return attended[None], grad_cells[None], lax.psum(bias_grad, "mp")


def solution(mesh):
    in_specs = (
        P("mp", "seq", None),
        P("mp", None),
        P("mp", None, None),
        P("mp", None, None),
        P(),
        P("mp", "seq", None),
    )
    out_specs = (P("mp", "seq", None), P("mp", "seq", None), P("seq", None))
    return jax.shard_map(shards, mesh=mesh, in_specs=in_specs, out_specs=out_specs, check_vma=False)
```

```python
import functools
import math

import jax
import jax.numpy as jnp
from jax import lax
from jax.experimental import pallas as pl
from jax.experimental.pallas import tpu as pltpu
from jax.sharding import PartitionSpec as P

HEADS = 16
HEAD_DIM = 128
ROW_BLOCKS = 4
VMEM_LIMIT = 56 * 1024 * 1024


def source_slots(owner_all, slot_count):
    position = jnp.arange(owner_all.shape[0], dtype=jnp.int32)
    same = owner_all[:, None] == owner_all[None, :]
    earlier = position[None, :] < position[:, None]
    return owner_all * slot_count + jnp.sum((same & earlier).astype(jnp.int32), axis=1)


def pack_kernel(slots, q_ref, k_ref, v_ref, g_ref, out_ref):
    out_ref[0, 0:slots, :] = q_ref[...]
    out_ref[0, slots : 2 * slots, :] = k_ref[...]
    out_ref[0, 2 * slots : 3 * slots, :] = v_ref[...]
    out_ref[0, 3 * slots :, :] = g_ref[...]


def pack(cells, grads, head, per_dev, num_dev):
    slots, tok = cells.shape[0], grads.shape[0]

    def part(j):
        return pl.BlockSpec((slots, HEAD_DIM), lambda d: (0, j * HEADS + d * per_dev + head))

    return pl.pallas_call(
        functools.partial(pack_kernel, slots),
        grid=(num_dev,),
        in_specs=[
            part(0),
            part(1),
            part(2),
            pl.BlockSpec((tok, HEAD_DIM), lambda d: (0, d * per_dev + head)),
        ],
        out_specs=pl.BlockSpec((1, 3 * slots + tok, HEAD_DIM), lambda d: (d, 0, 0)),
        out_shape=jax.ShapeDtypeStruct((num_dev, 3 * slots + tok, HEAD_DIM), jnp.bfloat16),
        compiler_params=pltpu.CompilerParams(vmem_limit_bytes=VMEM_LIMIT),
        cost_estimate=pl.CostEstimate(
            flops=0, bytes_accessed=4 * num_dev * (3 * slots + tok) * HEAD_DIM, transcendentals=0
        ),
    )(cells, cells, cells, grads)


def unpack_kernel(per_dev, *refs):
    cell_parts, out_parts = refs[:per_dev], refs[per_dev : 2 * per_dev]
    cells_ref, attended_ref = refs[2 * per_dev :]
    for s in range(cell_parts[0].shape[0]):
        for h in range(per_dev):
            cols = slice((s * per_dev + h) * HEAD_DIM, (s * per_dev + h + 1) * HEAD_DIM)
            cells_ref[:, cols] = cell_parts[h][s]
            attended_ref[:, cols] = out_parts[h][s]


def unpack(arrived, slots, tok):
    per_dev, num_dev = len(arrived), arrived[0].shape[0]
    group = math.gcd(num_dev, 4)
    steps = num_dev // group
    width = group * per_dev * HEAD_DIM
    last = 3 * slots // tok
    return pl.pallas_call(
        functools.partial(unpack_kernel, per_dev),
        grid=(steps, 3),
        in_specs=[pl.BlockSpec((group, slots, HEAD_DIM), lambda s, j: (s, j, 0))] * per_dev
        + [pl.BlockSpec((group, tok, HEAD_DIM), lambda s, j: (s, last, 0))] * per_dev,
        out_specs=[
            pl.BlockSpec((slots, width), lambda s, j: (0, j * steps + s)),
            pl.BlockSpec((tok, width), lambda s, j: (0, s)),
        ],
        out_shape=[
            jax.ShapeDtypeStruct((slots, 3 * steps * width), jnp.bfloat16),
            jax.ShapeDtypeStruct((tok, steps * width), jnp.bfloat16),
        ],
        compiler_params=pltpu.CompilerParams(vmem_limit_bytes=VMEM_LIMIT),
        cost_estimate=pl.CostEstimate(
            flops=0, bytes_accessed=4 * (3 * slots + tok) * steps * width, transcendentals=0
        ),
    )(*arrived, *arrived)


def dot(a, b, dims):
    return lax.dot_general(a, b, (dims, ((), ())), preferred_element_type=jnp.float32)


def attend_kernel(
    slots, tok, sel_ref, bias_ref, in_ref, col_ref, row_ref, out_ref, sum_ref,
    cells, qkv, ksel, vsel, dkey, dval, grads,
):
    num_dev = in_ref.shape[0]
    num_blocks, num_sel = sel_ref.shape
    total = num_dev * slots
    dim = HEAD_DIM
    scaling = 1.0 / math.sqrt(dim)

    @pl.loop(0, num_dev)
    def _(o):
        start = pl.multiple_of(o * slots, slots)
        for j in range(3):
            cells[pl.ds(start, slots), j * dim : (j + 1) * dim] = in_ref[
                o, j * slots : (j + 1) * slots, :
            ]

    @pl.loop(0, num_blocks)
    def _(b):
        rows = pl.ds(pl.multiple_of(b * tok, tok), tok)
        ids = lax.broadcasted_iota(jnp.int32, (tok, total), 1)
        hot = jnp.where(ids == col_ref[rows, :], 1.0, 0.0).astype(jnp.bfloat16)
        qkv[rows, :] = dot(hot, cells[...], ((1,), (0,))).astype(jnp.bfloat16)

    dkey[...] = jnp.zeros_like(dkey)
    dval[...] = jnp.zeros_like(dval)
    sum_ref[...] = jnp.zeros_like(sum_ref)
    kind = lax.broadcasted_iota(jnp.int32, (1, num_sel * tok), 1) >= ROW_BLOCKS * tok
    offset = jnp.where(kind, bias_ref[0, 1], bias_ref[0, 0])

    @pl.loop(0, num_blocks)
    def _(b):
        rows = pl.ds(pl.multiple_of(b * tok, tok), tok)
        query = qkv[rows, 0:dim]
        grad = in_ref[b, 3 * slots :, :]
        for i in range(num_sel):
            chosen = pl.ds(pl.multiple_of(sel_ref[b, i] * tok, tok), tok)
            ksel[i * tok : (i + 1) * tok, :] = qkv[chosen, dim : 2 * dim]
            vsel[i * tok : (i + 1) * tok, :] = qkv[chosen, 2 * dim : 3 * dim]
        scores = dot(query, ksel[...], ((1,), (1,))) * scaling + offset
        exps = jnp.exp(scores - jnp.max(scores, axis=1, keepdims=True))
        probs = exps * (1.0 / jnp.sum(exps, axis=1, keepdims=True))
        low = probs.astype(jnp.bfloat16)
        result = dot(low, vsel[...], ((1,), (0,))).astype(jnp.bfloat16)
        out_ref[b, 3 * slots :, :] = result
        delta = jnp.sum(
            grad.astype(jnp.float32) * result.astype(jnp.float32), axis=1, keepdims=True
        )
        dscore = probs * (dot(grad, vsel[...], ((1,), (1,))) - delta)
        sum_ref[...] += jnp.sum(dscore.reshape(tok // 8, 8, num_sel * tok), axis=0)
        dlow = dscore.astype(jnp.bfloat16)
        grads[rows, 0:dim] = (dot(dlow, ksel[...], ((1,), (0,))) * scaling).astype(jnp.bfloat16)
        dk = dot(dlow, query, ((0,), (0,))) * scaling
        dv = dot(low, grad, ((0,), (0,)))
        for i in range(num_sel):
            chosen = pl.ds(pl.multiple_of(sel_ref[b, i] * tok, tok), tok)
            dkey[chosen, :] += dk[i * tok : (i + 1) * tok, :]
            dval[chosen, :] += dv[i * tok : (i + 1) * tok, :]

    grads[:, dim : 2 * dim] = dkey[...].astype(jnp.bfloat16)
    grads[:, 2 * dim : 3 * dim] = dval[...].astype(jnp.bfloat16)

    @pl.loop(0, num_dev)
    def _(o):
        ids = lax.broadcasted_iota(jnp.int32, (slots, num_blocks * tok), 0) + o * slots
        hot = jnp.where(ids == row_ref[...], 1.0, 0.0).astype(jnp.bfloat16)
        back = dot(hot, grads[...], ((1,), (0,))).astype(jnp.bfloat16)
        for j in range(3):
            out_ref[o, j * slots : (j + 1) * slots, :] = back[:, j * dim : (j + 1) * dim]


def attend(arrived, source, selected, bias_pair, slots, tok):
    num_dev = arrived.shape[0]
    num_sel = selected.shape[1]
    length = source.shape[0]
    vmem = pl.BlockSpec(memory_space=pltpu.VMEM)
    smem = pl.BlockSpec(memory_space=pltpu.SMEM)
    dim = HEAD_DIM
    flops = 12 * length * num_sel * tok * dim + 12 * length * num_dev * slots * dim
    return pl.pallas_call(
        functools.partial(attend_kernel, slots, tok),
        in_specs=[smem, smem, vmem, vmem, vmem],
        out_specs=[vmem, vmem],
        out_shape=[
            jax.ShapeDtypeStruct(arrived.shape, jnp.bfloat16),
            jax.ShapeDtypeStruct((8, num_sel * tok), jnp.float32),
        ],
        scratch_shapes=[
            pltpu.VMEM((num_dev * slots, 3 * dim), jnp.bfloat16),
            pltpu.VMEM((length, 3 * dim), jnp.bfloat16),
            pltpu.VMEM((num_sel * tok, dim), jnp.bfloat16),
            pltpu.VMEM((num_sel * tok, dim), jnp.bfloat16),
            pltpu.VMEM((length, dim), jnp.float32),
            pltpu.VMEM((length, dim), jnp.float32),
            pltpu.VMEM((length, 3 * dim), jnp.bfloat16),
        ],
        compiler_params=pltpu.CompilerParams(vmem_limit_bytes=VMEM_LIMIT),
        cost_estimate=pl.CostEstimate(
            flops=2 * flops,
            bytes_accessed=4 * arrived.size,
            transcendentals=length * num_sel * tok,
        ),
    )(selected, bias_pair, arrived, source[:, None], source[None, :])


def exchange(array):
    return lax.all_to_all(array, "seq", split_axis=0, concat_axis=0, tiled=True)


def shards(qkv_owned, owner, band_rows, band_cols, bias, grad_out):
    num_dev = lax.axis_size("seq")
    my_index = lax.axis_index("seq")
    slots = qkv_owned.shape[1]
    tok = grad_out.shape[1]
    per_dev = HEADS // num_dev
    cells, grads = qkv_owned[0], grad_out[0]
    arrived = [exchange(pack(cells, grads, h, per_dev, num_dev)) for h in range(per_dev)]
    source = source_slots(owner[0], slots)
    selected = jnp.concatenate([band_rows[0], band_cols[0]], axis=1)
    bias_pair = lax.dynamic_slice_in_dim(bias, my_index * per_dev, per_dev, 0)
    back, sums = [], []
    for h in range(per_dev):
        out, part = attend(arrived[h], source, selected, bias_pair[h : h + 1], slots, tok)
        back.append(exchange(out))
        sums.append(part)
    sums = jnp.stack(sums)
    bias_grad = jnp.stack(
        [
            jnp.sum(sums[:, :, : ROW_BLOCKS * tok], axis=(1, 2)),
            jnp.sum(sums[:, :, ROW_BLOCKS * tok :], axis=(1, 2)),
        ],
        axis=1,
    )
    grad_cells, attended = unpack(back, slots, tok)
    return attended[None], grad_cells[None], lax.psum(bias_grad, "mp")


def solution(mesh):
    in_specs = (
        P("mp", "seq", None),
        P("mp", None),
        P("mp", None, None),
        P("mp", None, None),
        P(),
        P("mp", "seq", None),
    )
    out_specs = (P("mp", "seq", None), P("mp", "seq", None), P("seq", None))
    return jax.shard_map(shards, mesh=mesh, in_specs=in_specs, out_specs=out_specs, check_vma=False)
```

```python
import functools
import math

import jax
import jax.numpy as jnp
from jax import lax
from jax.experimental import pallas as pl
from jax.experimental.pallas import tpu as pltpu
from jax.sharding import PartitionSpec as P

HEADS = 16
HEAD_DIM = 128
ROW_BLOCKS = 4
VMEM_LIMIT = 56 * 1024 * 1024


def source_slots(owner_all, slot_count):
    position = jnp.arange(owner_all.shape[0], dtype=jnp.int32)
    same = owner_all[:, None] == owner_all[None, :]
    earlier = position[None, :] < position[:, None]
    return owner_all * slot_count + jnp.sum((same & earlier).astype(jnp.int32), axis=1)


def pack_kernel(slots, per_dev, head, cells_ref, grads_ref, out_ref, sems):
    num_dev = out_ref.shape[0]
    copies = []
    for d in range(num_dev):
        for j in range(4):
            col = d * per_dev + head
            if j < 3:
                col += j * HEADS
                source, rows = cells_ref, pl.ds(j * slots, slots)
            else:
                source, rows = grads_ref, pl.ds(3 * slots, grads_ref.shape[0])
            copies.append(
                pltpu.make_async_copy(
                    source.at[:, pl.ds(col * HEAD_DIM, HEAD_DIM)], out_ref.at[d, rows], sems.at[d, j]
                )
            )
    for copy in copies:
        copy.start()
    for copy in copies:
        copy.wait()


def pack(cells, grads, head, per_dev, num_dev):
    slots, tok = cells.shape[0], grads.shape[0]
    hbm = pl.BlockSpec(memory_space=pl.ANY)
    return pl.pallas_call(
        functools.partial(pack_kernel, slots, per_dev, head),
        in_specs=[hbm, hbm],
        out_specs=hbm,
        out_shape=jax.ShapeDtypeStruct((num_dev, 3 * slots + tok, HEAD_DIM), jnp.bfloat16),
        scratch_shapes=[pltpu.SemaphoreType.DMA((num_dev, 4))],
        compiler_params=pltpu.CompilerParams(vmem_limit_bytes=VMEM_LIMIT),
        cost_estimate=pl.CostEstimate(
            flops=0, bytes_accessed=4 * num_dev * (3 * slots + tok) * HEAD_DIM, transcendentals=0
        ),
    )(cells, grads)


def unpack_kernel(per_dev, *refs):
    cell_parts, out_parts = refs[:per_dev], refs[per_dev : 2 * per_dev]
    cells_ref, attended_ref = refs[2 * per_dev :]
    for s in range(cell_parts[0].shape[0]):
        for h in range(per_dev):
            cols = slice((s * per_dev + h) * HEAD_DIM, (s * per_dev + h + 1) * HEAD_DIM)
            cells_ref[:, cols] = cell_parts[h][s]
            attended_ref[:, cols] = out_parts[h][s]


def unpack(arrived, slots, tok):
    per_dev, num_dev = len(arrived), arrived[0].shape[0]
    group = math.gcd(num_dev, 4)
    steps = num_dev // group
    width = group * per_dev * HEAD_DIM
    last = 3 * slots // tok
    return pl.pallas_call(
        functools.partial(unpack_kernel, per_dev),
        grid=(steps, 3),
        in_specs=[pl.BlockSpec((group, slots, HEAD_DIM), lambda s, j: (s, j, 0))] * per_dev
        + [pl.BlockSpec((group, tok, HEAD_DIM), lambda s, j: (s, last, 0))] * per_dev,
        out_specs=[
            pl.BlockSpec((slots, width), lambda s, j: (0, j * steps + s)),
            pl.BlockSpec((tok, width), lambda s, j: (0, s)),
        ],
        out_shape=[
            jax.ShapeDtypeStruct((slots, 3 * steps * width), jnp.bfloat16),
            jax.ShapeDtypeStruct((tok, steps * width), jnp.bfloat16),
        ],
        compiler_params=pltpu.CompilerParams(vmem_limit_bytes=VMEM_LIMIT),
        cost_estimate=pl.CostEstimate(
            flops=0, bytes_accessed=4 * (3 * slots + tok) * steps * width, transcendentals=0
        ),
    )(*arrived, *arrived)


def dot(a, b, dims):
    return lax.dot_general(a, b, (dims, ((), ())), preferred_element_type=jnp.float32)


def attend_kernel(
    slots, tok, sel_ref, bias_ref, in_ref, col_ref, row_ref, out_ref, sum_ref,
    cells, qkv, ksel, vsel, dkey, dval, grads,
):
    num_dev = in_ref.shape[0]
    num_blocks, num_sel = sel_ref.shape
    total = num_dev * slots
    dim = HEAD_DIM
    scaling = 1.0 / math.sqrt(dim)

    @pl.loop(0, num_dev)
    def _(o):
        start = pl.multiple_of(o * slots, slots)
        for j in range(3):
            cells[pl.ds(start, slots), j * dim : (j + 1) * dim] = in_ref[
                o, j * slots : (j + 1) * slots, :
            ]

    @pl.loop(0, num_blocks)
    def _(b):
        rows = pl.ds(pl.multiple_of(b * tok, tok), tok)
        ids = lax.broadcasted_iota(jnp.int32, (tok, total), 1)
        hot = jnp.where(ids == col_ref[rows, :], 1.0, 0.0).astype(jnp.bfloat16)
        qkv[rows, :] = dot(hot, cells[...], ((1,), (0,))).astype(jnp.bfloat16)

    dkey[...] = jnp.zeros_like(dkey)
    dval[...] = jnp.zeros_like(dval)
    sum_ref[...] = jnp.zeros_like(sum_ref)
    kind = lax.broadcasted_iota(jnp.int32, (1, num_sel * tok), 1) >= ROW_BLOCKS * tok
    offset = jnp.where(kind, bias_ref[0, 1], bias_ref[0, 0])

    @pl.loop(0, num_blocks)
    def _(b):
        rows = pl.ds(pl.multiple_of(b * tok, tok), tok)
        query = qkv[rows, 0:dim]
        grad = in_ref[b, 3 * slots :, :]
        for i in range(num_sel):
            chosen = pl.ds(pl.multiple_of(sel_ref[b, i] * tok, tok), tok)
            ksel[i * tok : (i + 1) * tok, :] = qkv[chosen, dim : 2 * dim]
            vsel[i * tok : (i + 1) * tok, :] = qkv[chosen, 2 * dim : 3 * dim]
        scores = dot(query, ksel[...], ((1,), (1,))) * scaling + offset
        exps = jnp.exp(scores - jnp.max(scores, axis=1, keepdims=True))
        probs = exps * (1.0 / jnp.sum(exps, axis=1, keepdims=True))
        low = probs.astype(jnp.bfloat16)
        result = dot(low, vsel[...], ((1,), (0,))).astype(jnp.bfloat16)
        out_ref[b, 3 * slots :, :] = result
        delta = jnp.sum(
            grad.astype(jnp.float32) * result.astype(jnp.float32), axis=1, keepdims=True
        )
        dscore = probs * (dot(grad, vsel[...], ((1,), (1,))) - delta)
        sum_ref[...] += jnp.sum(dscore.reshape(tok // 8, 8, num_sel * tok), axis=0)
        dlow = dscore.astype(jnp.bfloat16)
        grads[rows, 0:dim] = (dot(dlow, ksel[...], ((1,), (0,))) * scaling).astype(jnp.bfloat16)
        dk = dot(dlow, query, ((0,), (0,))) * scaling
        dv = dot(low, grad, ((0,), (0,)))
        for i in range(num_sel):
            chosen = pl.ds(pl.multiple_of(sel_ref[b, i] * tok, tok), tok)
            dkey[chosen, :] += dk[i * tok : (i + 1) * tok, :]
            dval[chosen, :] += dv[i * tok : (i + 1) * tok, :]

    grads[:, dim : 2 * dim] = dkey[...].astype(jnp.bfloat16)
    grads[:, 2 * dim : 3 * dim] = dval[...].astype(jnp.bfloat16)

    @pl.loop(0, num_dev)
    def _(o):
        ids = lax.broadcasted_iota(jnp.int32, (slots, num_blocks * tok), 0) + o * slots
        hot = jnp.where(ids == row_ref[...], 1.0, 0.0).astype(jnp.bfloat16)
        back = dot(hot, grads[...], ((1,), (0,))).astype(jnp.bfloat16)
        for j in range(3):
            out_ref[o, j * slots : (j + 1) * slots, :] = back[:, j * dim : (j + 1) * dim]


def attend(arrived, source, selected, bias_pair, slots, tok):
    num_dev = arrived.shape[0]
    num_sel = selected.shape[1]
    length = source.shape[0]
    vmem = pl.BlockSpec(memory_space=pltpu.VMEM)
    smem = pl.BlockSpec(memory_space=pltpu.SMEM)
    dim = HEAD_DIM
    flops = 12 * length * num_sel * tok * dim + 12 * length * num_dev * slots * dim
    return pl.pallas_call(
        functools.partial(attend_kernel, slots, tok),
        in_specs=[smem, smem, vmem, vmem, vmem],
        out_specs=[vmem, vmem],
        out_shape=[
            jax.ShapeDtypeStruct(arrived.shape, jnp.bfloat16),
            jax.ShapeDtypeStruct((8, num_sel * tok), jnp.float32),
        ],
        scratch_shapes=[
            pltpu.VMEM((num_dev * slots, 3 * dim), jnp.bfloat16),
            pltpu.VMEM((length, 3 * dim), jnp.bfloat16),
            pltpu.VMEM((num_sel * tok, dim), jnp.bfloat16),
            pltpu.VMEM((num_sel * tok, dim), jnp.bfloat16),
            pltpu.VMEM((length, dim), jnp.float32),
            pltpu.VMEM((length, dim), jnp.float32),
            pltpu.VMEM((length, 3 * dim), jnp.bfloat16),
        ],
        compiler_params=pltpu.CompilerParams(vmem_limit_bytes=VMEM_LIMIT),
        cost_estimate=pl.CostEstimate(
            flops=2 * flops,
            bytes_accessed=4 * arrived.size,
            transcendentals=length * num_sel * tok,
        ),
    )(selected, bias_pair, arrived, source[:, None], source[None, :])


def exchange(array):
    return lax.all_to_all(array, "seq", split_axis=0, concat_axis=0, tiled=True)


def shards(qkv_owned, owner, band_rows, band_cols, bias, grad_out):
    num_dev = lax.axis_size("seq")
    my_index = lax.axis_index("seq")
    slots = qkv_owned.shape[1]
    tok = grad_out.shape[1]
    per_dev = HEADS // num_dev
    cells, grads = qkv_owned[0], grad_out[0]
    arrived = [exchange(pack(cells, grads, h, per_dev, num_dev)) for h in range(per_dev)]
    source = source_slots(owner[0], slots)
    selected = jnp.concatenate([band_rows[0], band_cols[0]], axis=1)
    bias_pair = lax.dynamic_slice_in_dim(bias, my_index * per_dev, per_dev, 0)
    back, sums = [], []
    for h in range(per_dev):
        out, part = attend(arrived[h], source, selected, bias_pair[h : h + 1], slots, tok)
        back.append(exchange(out))
        sums.append(part)
    sums = jnp.stack(sums)
    bias_grad = jnp.stack(
        [
            jnp.sum(sums[:, :, : ROW_BLOCKS * tok], axis=(1, 2)),
            jnp.sum(sums[:, :, ROW_BLOCKS * tok :], axis=(1, 2)),
        ],
        axis=1,
    )
    grad_cells, attended = unpack(back, slots, tok)
    return attended[None], grad_cells[None], lax.psum(bias_grad, "mp")


def solution(mesh):
    in_specs = (
        P("mp", "seq", None),
        P("mp", None),
        P("mp", None, None),
        P("mp", None, None),
        P(),
        P("mp", "seq", None),
    )
    out_specs = (P("mp", "seq", None), P("mp", "seq", None), P("seq", None))
    return jax.shard_map(shards, mesh=mesh, in_specs=in_specs, out_specs=out_specs, check_vma=False)
```
